256 devices in a mesh: grp: 8 (over z), lvl: 32 (over x, y, core).
Axes of the slice: x: 4, y: 4, z: 8, core: 2. Of those that a mesh axis runs over, the one named last changes fastest.
Arguments:
- vectors: bfloat16 [524288, 384], P(('grp', 'lvl')), may hold values from -6 to 6
- leaf_in: bfloat16 [256, 524288], P(None, ('grp', 'lvl')), may hold values from -0.125 to 0.125
- leaf_out: bfloat16 [524288, 256], P(('grp', 'lvl')), may hold values from -0.375 to 0.375
- factors: bfloat16 [256, 8, 2, 256, 256], P(('grp', 'lvl')), may hold values from -0.25 to 0.25
- dense_rows: bfloat16 [1536, 524288], P(None, ('grp', 'lvl')), may hold values from -0.03125 to 0.03125
- sample_rows: int32 [1536], P(('grp', 'lvl')), may hold values from 0 to 2047
Outputs:
- residual: float32 [1536, 384], P(('grp', 'lvl'))
The draws below stay inside these ranges and needn't reach their ends.
Inputs may be any that keep to these rules, and one draw needn't show every extreme that they name: `sample_rows`: sample m indexes a row of box m // 6.
All inputs are finite; a program needn't handle non-finite values.
Results may differ from the reference program's by a relative error of at most 0.019.
Values may be sent and summed in bfloat16 or wider, within the bound.
A program may use at most 128 MiB of HBM per device.

```python
import jax
import jax.numpy as jnp
from jax import lax

ROWS_DEV = 2048
R = 256
V = 384
SAMP_DEV = 6
LEVELS = 8
N = 524288
M = 1536
DEVICES = 256


def touch_ends(drawn, key, least, top_value):
    longest = drawn.shape.index(max(drawn.shape))
    spots = []
    for shift in (0, 1):
        where = [jax.random.randint(jax.random.fold_in(key, axis), (), 0, length) for axis, length in enumerate(drawn.shape)]
        where[longest] = (where[longest] + shift) % drawn.shape[longest]
        spots.append(tuple(where))
    return drawn.at[spots[0]].set(least).at[spots[1]].set(top_value)


def spiked(result, own_key, source, target, parts, factor):
    def block_of(axis_at):
        return (jnp.arange(result.shape[axis_at]) // (result.shape[axis_at] // parts)).reshape((-1,) + (1,) * (result.ndim - 1 - axis_at))

    first = jax.random.permutation(own_key, parts)[block_of(target)]
    second = (block_of(target) + parts // 2) % parts
    return jnp.where((block_of(source) == first) | (block_of(source) == second), factor * result, result)


def block_scale(stream_key, shape, pieces, low, high):
    def one(dim, shards_of):
        steps = jax.random.uniform(jax.random.fold_in(jax.random.fold_in(stream_key, 6), dim), (shards_of,), jnp.float32, low / len(pieces), high / len(pieces))
        return jnp.repeat(jnp.exp(steps), shape[dim] // shards_of).reshape((-1,) + (1,) * (len(shape) - dim - 1))

    level = one(*pieces[0])
    for cut in pieces[1:]:
        level = level * one(*cut)
    return level


def gaussian(own_key, shape, spread, bound, pieces=(), kind=jnp.bfloat16):
    drawn = jax.random.normal(own_key, shape, jnp.float32) * spread
    if len(pieces) > 0:
        drawn = block_scale(own_key, shape, pieces, -0.22, 0.18) * drawn
    return jnp.clip(drawn, min=-bound, max=bound).astype(kind)


def heavy_noise(rng, dims, deviation, bound, pieces, heavy, kind=jnp.bfloat16):
    result = deviation * jax.random.normal(rng, dims, jnp.float32)
    if pieces:
        result = result * block_scale(rng, dims, pieces, -0.22, 0.18)
    return jnp.clip(spiked(result, jax.random.fold_in(rng, 3), *heavy), -bound, bound).astype(kind)


def setup_inputs(seed: int = 0) -> dict:
    key_list = jax.random.split(jax.random.key(seed), 7)
    return {
        "vectors": gaussian(key_list[0], (N, V), 1.0, 6.0, ((0, 256),)),
        "leaf_in": gaussian(key_list[1], (R, N), ROWS_DEV ** -0.5, 0.125, ((1, 256),)),
        "leaf_out": gaussian(key_list[2], (N, R), R ** -0.5, 0.375, ((0, 256),)),
        "factors": gaussian(key_list[3], (DEVICES, LEVELS, 2, R, R), (2 * R) ** -0.5, 0.25, ((0, 256),)),
        "dense_rows": heavy_noise(key_list[4], (M, N), (ROWS_DEV * DEVICES) ** -0.5, 0.03125, ((1, 256),), (1, 0, 256, 6.0)),
        "sample_rows": touch_ends(jax.random.randint(key_list[5], (M,), 0, ROWS_DEV), jax.random.fold_in(key_list[5], 1), 0, ROWS_DEV - 1).astype(jnp.int32),
    }


def leaf_product(operands):
    return jnp.dot(operands[0], operands[1], preferred_element_type=jnp.float32).astype(jnp.bfloat16)


def reference(vectors, leaf_in, leaf_out, factors, dense_rows, sample_rows):
    blocks_in = leaf_in.reshape(R, DEVICES, ROWS_DEV).transpose(1, 0, 2)
    vector_blocks = vectors.reshape(DEVICES, ROWS_DEV, V)
    coefficients = lax.map(leaf_product, (blocks_in, vector_blocks))
    for step_index in range(LEVELS):
        half_span = 2 ** step_index
        opposite = coefficients.reshape(DEVICES // (2 * half_span), 2, half_span, R, V)[:, ::-1].reshape(DEVICES, R, V)
        level_factors = factors[:, step_index].astype(jnp.float32)
        mixed = jnp.einsum("drs,dsv->drv", level_factors[:, 0], coefficients.astype(jnp.float32))
        mixed = mixed + jnp.einsum("drs,dsv->drv", level_factors[:, 1], opposite.astype(jnp.float32))
        coefficients = mixed.astype(jnp.bfloat16)
    owners = jnp.arange(M, dtype=jnp.int32) // SAMP_DEV
    global_rows = (owners * ROWS_DEV + sample_rows).astype(jnp.int32)
    picked = leaf_out[global_rows].astype(jnp.float32).reshape(DEVICES, SAMP_DEV, R)
    estimate = jnp.einsum("dsr,drv->dsv", picked, coefficients.astype(jnp.float32)).reshape(M, V)
    exact = jnp.dot(dense_rows, vectors, preferred_element_type=jnp.float32)
    return estimate - exact
```

```python
import functools

import jax
import jax.numpy as jnp
from jax import lax
from jax.experimental import pallas as pl
from jax.experimental.pallas import tpu as pltpu
from jax.sharding import PartitionSpec as P

MESH = pl.DeviceIdType.MESH
BF16, F32 = jnp.bfloat16, jnp.float32

ROWS, RANK, VECS, SAMP = 2048, 256, 384, 6
Z, X, Y = 8, 4, 4
BLOCK = Z * SAMP
HALF = Y * BLOCK
CHUNK = 128
CHUNKS = VECS // CHUNK
PAD = 16
GROUPS = (0, 4, 2, 6, 1, 5, 3, 7)


def dot(a, b):
    return jnp.dot(a, b, preferred_element_type=F32)


def dot16(a, b):
    return dot(a, b).astype(BF16)


def count_steps(values, step, steps):
    total = jnp.zeros_like(values)
    for i in range(1, steps):
        total = total + (values >= i * step).astype(jnp.int32)
    return total


def permutation(core, y):
    row = lax.broadcasted_iota(jnp.int32, (2 * HALF, 1), 0)
    half = count_steps(row, HALF, 2)
    row = row - half * HALF
    quarter = count_steps(row, BLOCK, Y)
    row = row - quarter * BLOCK
    z = count_steps(row, SAMP, Z)
    sample = row - z * SAMP
    source = z * BLOCK + (quarter ^ y) * (2 * SAMP) + (half ^ core) * SAMP + sample
    column = lax.broadcasted_iota(jnp.int32, (2 * HALF, 2 * HALF), 1)
    return jnp.where(column == source, 1.0, 0.0).astype(BF16)


def spread(z):
    row = lax.broadcasted_iota(jnp.int32, (Z * PAD, 1), 0)
    group = count_steps(row, PAD, Z)
    sample = row - group * PAD
    offset = jnp.zeros_like(group)
    for i, value in enumerate(GROUPS):
        offset = offset + jnp.where(group == i, value, 0)
    source = jnp.where(sample < SAMP, (offset ^ z) * SAMP + sample, -1)
    column = lax.broadcasted_iota(jnp.int32, (Z * PAD, BLOCK), 1)
    return jnp.where(column == source, 1.0, 0.0).astype(BF16)


def kernel(
    samp, vec_hbm, lin_hbm, lout_hbm, fac_hbm, dense_hbm, out,
    vec, lin, lout, fac, dense, perm,
    c0_send, c0_recv, far_y, far_x, c1, y_recv, c3, x_recv,
    half_send, half_recv, mine, xs_send, xs_recv, ys_send, ys_recv, total_y,
    w_send4, w_recv4, w_send2, w_recv2, w_send1, w_recv1, w_all, exact,
    tail_send, tail_recv, local_sem, send_sem, recv_sem,
):
    z, lvl = lax.axis_index("grp"), lax.axis_index("lvl")
    x, y, core = lvl // 8, (lvl // 2) % 4, lvl % 2

    def core_peer():
        return (z, lvl ^ 1)

    def y_peer(j):
        return (z, lvl ^ (2 * j))

    def x_peer(j):
        return (z, lvl ^ (8 * j))

    def z_peer(j):
        return (z ^ j, lvl)

    peers = [core_peer()] + [y_peer(j) for j in (1, 2, 3)] + [x_peer(j) for j in (1, 2, 3)]
    peers += [z_peer(j) for j in range(1, Z)]
    barrier = pltpu.get_barrier_semaphore()
    for peer in peers:
        pl.semaphore_signal(barrier, inc=1, device_id=peer, device_id_type=MESH)

    used = [0, 0]
    sent = []

    def load(source, target):
        copy = pltpu.make_async_copy(source, target, local_sem.at[used[0]])
        used[0] += 1
        copy.start()
        return copy

    def send(source, target, peer):
        copy = pltpu.make_async_remote_copy(
            src_ref=source,
            dst_ref=target,
            send_sem=send_sem.at[used[1]],
            recv_sem=recv_sem.at[used[1]],
            device_id=peer,
            device_id_type=MESH,
        )
        used[1] += 1
        copy.start()
        sent.append(copy)
        return copy

    def load_factors(level):
        return load(fac_hbm.at[0, level], fac.at[level])

    def load_dense(j):
        copies = []
        for group in range(Z):
            first = pl.multiple_of(group * (X * BLOCK) + (x ^ j) * BLOCK, BLOCK)
            copies.append(
                load(dense_hbm.at[pl.ds(first, BLOCK), :], dense.at[j, pl.ds(group * BLOCK, BLOCK), :])
            )
        return copies

    got_lout = load(lout_hbm, lout)
    got_fac = {7: load_factors(7)}
    got_lin, got_vec = load(lin_hbm, lin), load(vec_hbm, vec)
    got_fac[0] = load_factors(0)
    got_dense = {}
    order = (1, 2, 3, 0)
    for j in order[:2]:
        got_dense[j] = load_dense(j)
    got_fac[6] = load_factors(6)
    for j in order[2:]:
        got_dense[j] = load_dense(j)
    for level in (1, 2, 5, 3, 4):
        got_fac[level] = load_factors(level)

    column = lax.broadcasted_iota(jnp.int32, (PAD, ROWS), 1)
    row = lax.broadcasted_iota(jnp.int32, (PAD, ROWS), 0)
    hot = jnp.zeros((PAD, ROWS), F32)
    for i in range(SAMP):
        hot = jnp.where((row == i) & (column == samp[i]), 1.0, hot)
    hot = hot.astype(BF16)
    got_lout.wait()
    w = dot16(hot, lout[...])
    got_fac[7].wait()
    w_send4[...] = dot16(w, fac[7, 1])
    own4 = dot16(w, fac[7, 0])

    perm[...] = permutation(core, y)

    got_lin.wait()
    got_vec.wait()
    c0_send[...] = dot16(lin[...], vec[...])

    pl.semaphore_wait(barrier, len(peers))
    move4 = send(w_send4, w_recv4, z_peer(4))
    move_c0 = send(c0_send, c0_recv, core_peer())
    move_far_y = send(fac_hbm.at[0, 1], far_y, y_peer(2))
    move_far_x = send(fac_hbm.at[0, 3], far_x, x_peer(2))

    def dense_product(j):
        for copy in got_dense[j]:
            copy.wait()
        product = dot16(dense[j], vec[...])
        product = dot(perm[...], product)
        mine[j] = product[:HALF]
        half_send[j] = product[HALF:].astype(BF16)
        return send(half_send.at[j], half_recv.at[j], core_peer())

    move_half = {}
    for j in (1, 2):
        move_half[j] = dense_product(j)

    got_fac[0].wait()
    move_c0.wait_recv()
    c1[...] = (dot(fac[0, 0], c0_send[...]) + dot(fac[0, 1], c0_recv[...])).astype(BF16)
    move_c1 = {}
    for k in range(CHUNKS):
        columns = pl.ds(k * CHUNK, CHUNK)
        for j in (2, 1, 3):
            move_c1[k, j] = send(c1.at[:, columns], y_recv.at[j - 1, :, columns], y_peer(j))

    for j in (3, 0):
        move_half[j] = dense_product(j)

    move_xs = {}
    for j in (1, 2, 3):
        move_half[j].wait_recv()
        xs_send[j - 1] = (mine[j] + half_recv[j].astype(F32)).astype(BF16)
        move_xs[j] = send(xs_send.at[j - 1], xs_recv.at[j - 1], x_peer(j))

    got_fac[6].wait()
    move4.wait_recv()
    w = jnp.concatenate([own4, w_recv4[...]], axis=0)
    w_send2[...] = dot16(w, fac[6, 1])
    move2 = send(w_send2, w_recv2, z_peer(2))
    own2 = dot16(w, fac[6, 0])

    def combine(level, far, near, others, columns):
        a = (dot(fac[level, 0], near) + dot(fac[level, 1], others[0, :, columns])).astype(BF16)
        b = (dot(far[0], others[1, :, columns]) + dot(far[1], others[2, :, columns])).astype(BF16)
        return (dot(fac[level + 1, 0], a) + dot(fac[level + 1, 1], b)).astype(BF16)

    for level in (1, 2, 5, 3, 4):
        got_fac[level].wait()
    move_far_y.wait_recv()
    move_c3 = {}

    def y_levels(k):
        columns = pl.ds(k * CHUNK, CHUNK)
        for j in (1, 2, 3):
            move_c1[k, j].wait_recv()
        c3[:, columns] = combine(1, far_y, c1[:, columns], y_recv, columns)
        for j in (2, 1, 3):
            move_c3[k, j] = send(c3.at[:, columns], x_recv.at[j - 1, :, columns], x_peer(j))

    y_levels(0)

    move2.wait_recv()
    w = jnp.concatenate([own2, w_recv2[...]], axis=0)
    w_send1[...] = dot16(w, fac[5, 1])
    move1 = send(w_send1, w_recv1, z_peer(1))
    w_all[: 4 * PAD] = dot16(w, fac[5, 0])

    y_levels(1)

    move_half[0].wait_recv()
    total = mine[0] + half_recv[0].astype(F32)
    for j in (1, 2, 3):
        move_xs[j].wait_recv()
        total = total + xs_recv[j - 1].astype(F32)
    total_y[...] = total[:BLOCK]
    move_ys = {}
    for j in (1, 2, 3):
        ys_send[j - 1] = total[j * BLOCK : (j + 1) * BLOCK].astype(BF16)
        move_ys[j] = send(ys_send.at[j - 1], ys_recv.at[j - 1], y_peer(j))

    y_levels(2)

    total = total_y[...]
    for j in (1, 2, 3):
        move_ys[j].wait_recv()
        total = total + ys_recv[j - 1].astype(F32)
    high = total.astype(BF16)
    low = (total - high.astype(F32)).astype(BF16)
    onto = spread(z)
    exact[...] = dot(onto, high) + dot(onto, low)

    move1.wait_recv()
    w_all[4 * PAD :] = w_recv1[...]
    move_far_x.wait_recv()

    move_tail = {}
    for k in range(CHUNKS):
        columns = pl.ds(k * CHUNK, CHUNK)
        for j in (1, 2, 3):
            move_c3[k, j].wait_recv()
        c5 = combine(3, far_x, c3[:, columns], x_recv, columns)
        part = dot(w_all[...], c5) - exact[:, columns]
        for i in range(Z):
            tail_send[k, i] = part[i * PAD : i * PAD + 8]
        for i in range(1, Z):
            move_tail[k, i] = send(tail_send.at[k, i], tail_recv.at[k, i], z_peer(GROUPS[i]))

    for k in range(CHUNKS):
        part = tail_send[k, 0]
        for i in range(1, Z):
            move_tail[k, i].wait_recv()
            part = part + tail_recv[k, i]
        out[:, pl.ds(k * CHUNK, CHUNK)] = part[:SAMP]
    for copy in sent:
        copy.wait_send()


LOCAL = 4 + 7 + Z * X
REMOTE = 4 + 4 + 2 * 3 * CHUNKS + 6 + 2 + (Z - 1) * CHUNKS


def per_device(vectors, leaf_in, leaf_out, factors, dense_rows, sample_rows):
    vmem = pltpu.VMEM
    scratch = [
        vmem((ROWS, VECS), BF16),
        vmem((RANK, ROWS), BF16),
        vmem((ROWS, RANK), BF16),
        vmem((8, 2, RANK, RANK), BF16),
        vmem((X, 2 * HALF, ROWS), BF16),
        vmem((2 * HALF, 2 * HALF), BF16),
        vmem((RANK, VECS), BF16),
        vmem((RANK, VECS), BF16),
        vmem((2, RANK, RANK), BF16),
        vmem((2, RANK, RANK), BF16),
        vmem((RANK, VECS), BF16),
        vmem((3, RANK, VECS), BF16),
        vmem((RANK, VECS), BF16),
        vmem((3, RANK, VECS), BF16),
        vmem((X, HALF, VECS), BF16),
        vmem((X, HALF, VECS), BF16),
        vmem((X, HALF, VECS), F32),
        vmem((3, HALF, VECS), BF16),
        vmem((3, HALF, VECS), BF16),
        vmem((3, BLOCK, VECS), BF16),
        vmem((3, BLOCK, VECS), BF16),
        vmem((BLOCK, VECS), F32),
        vmem((PAD, RANK), BF16),
        vmem((PAD, RANK), BF16),
        vmem((2 * PAD, RANK), BF16),
        vmem((2 * PAD, RANK), BF16),
        vmem((4 * PAD, RANK), BF16),
        vmem((4 * PAD, RANK), BF16),
        vmem((8 * PAD, RANK), BF16),
        vmem((8 * PAD, VECS), F32),
        vmem((CHUNKS, Z, 8, CHUNK), F32),
        vmem((CHUNKS, Z, 8, CHUNK), F32),
        pltpu.SemaphoreType.DMA((LOCAL,)),
        pltpu.SemaphoreType.DMA((REMOTE,)),
        pltpu.SemaphoreType.DMA((REMOTE,)),
    ]
    anywhere = pl.BlockSpec(memory_space=pl.ANY)
    return pl.pallas_call(
        kernel,
        out_shape=jax.ShapeDtypeStruct((SAMP, VECS), F32),
        in_specs=[pl.BlockSpec(memory_space=pltpu.SMEM)] + [anywhere] * 5,
        out_specs=pl.BlockSpec(memory_space=pltpu.VMEM),
        scratch_shapes=scratch,
        compiler_params=pltpu.CompilerParams(
            collective_id=0, has_side_effects=True, vmem_limit_bytes=56 * 2**20
        ),
        cost_estimate=pl.CostEstimate(
            flops=2 * 1700 * 10**6, bytes_accessed=12 * 2**20, transcendentals=0
        ),
    )(sample_rows, vectors, leaf_in, leaf_out, factors, dense_rows)


def solution(mesh):
    return jax.shard_map(
        per_device,
        mesh=mesh,
        in_specs=(
            P(("grp", "lvl"), None),
            P(None, ("grp", "lvl")),
            P(("grp", "lvl"), None),
            P(("grp", "lvl"), None, None, None, None),
            P(None, ("grp", "lvl")),
            P(("grp", "lvl")),
        ),
        out_specs=P(("grp", "lvl"), None),
        check_vma=False,
    )
```

```python
import functools

import jax
import jax.numpy as jnp
from jax import lax
from jax.experimental import pallas as pl
from jax.experimental.pallas import tpu as pltpu
from jax.sharding import PartitionSpec as P

MESH = pl.DeviceIdType.MESH
BF16, F32 = jnp.bfloat16, jnp.float32

ROWS, RANK, VECS, SAMP = 2048, 256, 384, 6
Z, X, Y = 8, 4, 4
BLOCK = Z * SAMP
HALF = Y * BLOCK
CHUNK = 128
CHUNKS = VECS // CHUNK
ROOM = 8
GROUPS = (0, 4, 2, 6, 1, 5, 3, 7)


def dot(a, b):
    return jnp.dot(a, b, preferred_element_type=F32)


def dot16(a, b):
    return dot(a, b).astype(BF16)


def count_steps(values, step, steps):
    total = jnp.zeros_like(values)
    for i in range(1, steps):
        total = total + (values >= i * step).astype(jnp.int32)
    return total


def permutation(core, y):
    row = lax.broadcasted_iota(jnp.int32, (2 * HALF, 1), 0)
    half = count_steps(row, HALF, 2)
    row = row - half * HALF
    quarter = count_steps(row, BLOCK, Y)
    row = row - quarter * BLOCK
    z = count_steps(row, SAMP, Z)
    sample = row - z * SAMP
    source = z * BLOCK + (quarter ^ y) * (2 * SAMP) + (half ^ core) * SAMP + sample
    column = lax.broadcasted_iota(jnp.int32, (2 * HALF, 2 * HALF), 1)
    return jnp.where(column == source, 1.0, 0.0).astype(BF16)


def spread(z):
    row = lax.broadcasted_iota(jnp.int32, (Z * ROOM, 1), 0)
    group = count_steps(row, ROOM, Z)
    sample = row - group * ROOM
    offset = jnp.zeros_like(group)
    for i, value in enumerate(GROUPS):
        offset = offset + jnp.where(group == i, value, 0)
    source = jnp.where(sample < SAMP, (offset ^ z) * SAMP + sample, -1)
    column = lax.broadcasted_iota(jnp.int32, (Z * ROOM, BLOCK), 1)
    return jnp.where(column == source, 1.0, 0.0).astype(BF16)


def kernel(
    samp, vec_hbm, lin_hbm, lout_hbm, fac_hbm, dense_hbm, out,
    vec, lin, lout, fac, dense, perm,
    c0_send, c0_recv, c1, c1_recv, c2, c2_recv, c3, c3_recv,
    half_send, half_recv, mine, xs_send, xs_recv, ys_send, ys_recv, total_y,
    w_send4, w_recv4, w_send2, w_recv2, w_send1, w_recv1, w_send_x, w_recv_x, w_all,
    tail_send, tail_recv, local_sem, send_sem, recv_sem,
):
    z, lvl = lax.axis_index("grp"), lax.axis_index("lvl")
    x, y, core = lvl // 8, (lvl // 2) % 4, lvl % 2

    def core_peer():
        return (z, lvl ^ 1)

    def y_peer(j):
        return (z, lvl ^ (2 * j))

    def x_peer(j):
        return (z, lvl ^ (8 * j))

    def z_peer(j):
        return (z ^ j, lvl)

    def tail_peer(i):
        return (z ^ GROUPS[i % Z], lvl ^ (16 * (i // Z)))

    peers = [core_peer()] + [y_peer(j) for j in (1, 2, 3)] + [x_peer(j) for j in (1, 3)]
    peers += [tail_peer(i) for i in range(1, 2 * Z)]
    barrier = pltpu.get_barrier_semaphore()
    for peer in peers:
        pl.semaphore_signal(barrier, inc=1, device_id=peer, device_id_type=MESH)

    used = [0, 0]
    sent = []

    def load(source, target):
        copy = pltpu.make_async_copy(source, target, local_sem.at[used[0]])
        used[0] += 1
        copy.start()
        return copy

    def send(source, target, peer):
        copy = pltpu.make_async_remote_copy(
            src_ref=source,
            dst_ref=target,
            send_sem=send_sem.at[used[1]],
            recv_sem=recv_sem.at[used[1]],
            device_id=peer,
            device_id_type=MESH,
        )
        used[1] += 1
        copy.start()
        sent.append(copy)
        return copy

    def load_factors(level):
        return load(fac_hbm.at[0, level], fac.at[level])

    def load_dense(j):
        copies = []
        for group in range(Z):
            first = pl.multiple_of(group * (X * BLOCK) + (x ^ j) * BLOCK, BLOCK)
            copies.append(
                load(dense_hbm.at[pl.ds(first, BLOCK), :], dense.at[j, pl.ds(group * BLOCK, BLOCK), :])
            )
        return copies

    got_lin, got_vec = load(lin_hbm, lin), load(vec_hbm, vec)
    got_lout = load(lout_hbm, lout)
    got_fac = {7: load_factors(7)}
    got_fac[0] = load_factors(0)
    got_dense = {}
    order = (2, 1, 3, 0)
    for j in order[:2]:
        got_dense[j] = load_dense(j)
    got_fac[1] = load_factors(1)
    got_fac[6] = load_factors(6)
    for j in order[2:]:
        got_dense[j] = load_dense(j)
    for level in (2, 5, 3, 4):
        got_fac[level] = load_factors(level)

    column = lax.broadcasted_iota(jnp.int32, (2 * ROOM, ROWS), 1)
    row = lax.broadcasted_iota(jnp.int32, (2 * ROOM, ROWS), 0)
    hot = jnp.zeros((2 * ROOM, ROWS), F32)
    for i in range(SAMP):
        hot = jnp.where((row == i) & (column == samp[i]), 1.0, hot)
    hot = hot.astype(BF16)
    perm[...] = permutation(core, y)

    got_lin.wait()
    got_vec.wait()
    c0_send[...] = dot16(lin[...], vec[...])

    got_lout.wait()
    w = dot16(hot, lout[...])
    got_fac[7].wait()
    w_send4[...] = dot16(w, fac[7, 1])
    own4 = dot(w, fac[7, 0])[:ROOM]

    pl.semaphore_wait(barrier, len(peers))
    move4 = send(w_send4, w_recv4, z_peer(4))
    move_c0 = send(c0_send, c0_recv, core_peer())

    def dense_product(j):
        for copy in got_dense[j]:
            copy.wait()
        product = dot16(dense[j], vec[...])
        product = dot(perm[...], product)
        mine[j] = product[:HALF]
        half_send[j] = product[HALF:].astype(BF16)
        return send(half_send.at[j], half_recv.at[j], core_peer())

    move_half = {2: dense_product(2)}
    got_fac[0].wait()
    near = dot(fac[0, 0], c0_send[...])
    move_c0.wait_recv()
    c1[...] = (near + dot(fac[0, 1], c0_recv[...])).astype(BF16)

    columns = [pl.ds(k * CHUNK, CHUNK) for k in range(CHUNKS)]

    def exchange(k, ref, landing, peer):
        return send(ref.at[:, columns[k]], landing.at[:, columns[k]], peer)

    def combine(level, k, ref, landing, move, result):
        near = dot(fac[level, 0], ref[:, columns[k]])
        move.wait_recv()
        far = dot(fac[level, 1], landing[:, columns[k]])
        result[:, columns[k]] = (near + far).astype(BF16)

    def send_half(j):
        move_half[j].wait_recv()
        xs_send[j - 1] = (mine[j] + half_recv[j].astype(F32)).astype(BF16)
        return send(xs_send.at[j - 1], xs_recv.at[j - 1], x_peer(j))

    move_c1 = [exchange(k, c1, c1_recv, y_peer(1)) for k in range(CHUNKS)]
    move_xs, move_c2, move_c3 = {}, {}, {}
    move_half[1] = dense_product(1)
    move_xs[2] = send_half(2)
    move_half[3] = dense_product(3)
    move_xs[1] = send_half(1)
    move_half[0] = dense_product(0)
    move_xs[3] = send_half(3)

    got_fac[6].wait()
    move4.wait_recv()
    w = jnp.concatenate([own4, w_recv4[...].astype(F32)[:ROOM]], axis=0).astype(BF16)
    w_send2[...] = dot16(w, fac[6, 1])
    move2 = send(w_send2, w_recv2, z_peer(2))
    own2 = dot16(w, fac[6, 0])

    got_fac[1].wait()
    for k in range(CHUNKS):
        combine(1, k, c1, c1_recv, move_c1[k], c2)
        move_c2[k] = exchange(k, c2, c2_recv, y_peer(2))

    got_fac[5].wait()
    move2.wait_recv()
    w = jnp.concatenate([own2, w_recv2[...]], axis=0)
    w_send1[...] = dot16(w, fac[5, 1])
    move1 = send(w_send1, w_recv1, z_peer(1))
    own1 = dot16(w, fac[5, 0])

    got_fac[2].wait()
    combine(2, 0, c2, c2_recv, move_c2[0], c3)
    move_c3[0] = exchange(0, c3, c3_recv, x_peer(1))

    got_fac[4].wait()
    move1.wait_recv()
    w = jnp.concatenate([own1, w_recv1[...]], axis=0)
    w_send_x[...] = dot16(w, fac[4, 1])
    move_x = send(w_send_x, w_recv_x, x_peer(2))
    w_all[: Z * ROOM] = dot16(w, fac[4, 0])

    combine(2, 1, c2, c2_recv, move_c2[1], c3)
    move_c3[1] = exchange(1, c3, c3_recv, x_peer(1))

    combine(2, 2, c2, c2_recv, move_c2[2], c3)
    move_c3[2] = exchange(2, c3, c3_recv, x_peer(1))

    move_half[0].wait_recv()
    total = mine[0] + half_recv[0].astype(F32)
    for j in (1, 2, 3):
        move_xs[j].wait_recv()
        total = total + xs_recv[j - 1].astype(F32)
    total_y[...] = total[:BLOCK]
    move_ys = {}
    for j in (1, 2, 3):
        ys_send[j - 1] = total[j * BLOCK : (j + 1) * BLOCK].astype(BF16)
        move_ys[j] = send(ys_send.at[j - 1], ys_recv.at[j - 1], y_peer(j))

    got_fac[3].wait()
    onto = spread(z)
    move_x.wait_recv()
    w_all[Z * ROOM :] = w_recv_x[...]
    w = w_all[...]

    move_tail = {}

    def send_tail(k, i):
        move_tail[k, i] = send(tail_send.at[k, i], tail_recv.at[k, i], tail_peer(i))

    for k in range(CHUNKS):
        near = dot(fac[3, 0], c3[:, columns[k]])
        move_c3[k].wait_recv()
        far = dot(fac[3, 1], c3_recv[:, columns[k]])
        part = dot(w, (near + far).astype(BF16))
        for i in range(2 * Z):
            tail_send[k, i] = part[i * ROOM : (i + 1) * ROOM]
        for i in range(Z, 2 * Z):
            send_tail(k, i)

    total = total_y[...]
    for j in (1, 2, 3):
        move_ys[j].wait_recv()
        total = total + ys_recv[j - 1].astype(F32)
    high = total.astype(BF16)
    low = (total - high.astype(F32)).astype(BF16)
    exact = dot(onto, high) + dot(onto, low)
    for i in range(Z):
        for k in range(CHUNKS):
            rows = exact[i * ROOM : (i + 1) * ROOM, k * CHUNK : (k + 1) * CHUNK]
            tail_send[k, i] = tail_send[k, i] - rows
            if i > 0:
                send_tail(k, i)

    for k in range(CHUNKS):
        part = tail_send[k, 0]
        for i in range(1, 2 * Z):
            move_tail[k, i].wait_recv()
            part = part + tail_recv[k, i]
        out[:, columns[k]] = part[:SAMP]
    for copy in sent:
        copy.wait_send()


LOCAL = 3 + 8 + Z * X
REMOTE = 1 + 3 * CHUNKS + 4 + 3 + 3 + 4 + (2 * Z - 1) * CHUNKS


def per_device(vectors, leaf_in, leaf_out, factors, dense_rows, sample_rows):
    vmem = pltpu.VMEM
    scratch = [
        vmem((ROWS, VECS), BF16),
        vmem((RANK, ROWS), BF16),
        vmem((ROWS, RANK), BF16),
        vmem((8, 2, RANK, RANK), BF16),
        vmem((X, 2 * HALF, ROWS), BF16),
        vmem((2 * HALF, 2 * HALF), BF16),
        vmem((RANK, VECS), BF16),
        vmem((RANK, VECS), BF16),
        vmem((RANK, VECS), BF16),
        vmem((RANK, VECS), BF16),
        vmem((RANK, VECS), BF16),
        vmem((RANK, VECS), BF16),
        vmem((RANK, VECS), BF16),
        vmem((RANK, VECS), BF16),
        vmem((X, HALF, VECS), BF16),
        vmem((X, HALF, VECS), BF16),
        vmem((X, HALF, VECS), F32),
        vmem((3, HALF, VECS), BF16),
        vmem((3, HALF, VECS), BF16),
        vmem((3, BLOCK, VECS), BF16),
        vmem((3, BLOCK, VECS), BF16),
        vmem((BLOCK, VECS), F32),
        vmem((2 * ROOM, RANK), BF16),
        vmem((2 * ROOM, RANK), BF16),
        vmem((2 * ROOM, RANK), BF16),
        vmem((2 * ROOM, RANK), BF16),
        vmem((4 * ROOM, RANK), BF16),
        vmem((4 * ROOM, RANK), BF16),
        vmem((8 * ROOM, RANK), BF16),
        vmem((8 * ROOM, RANK), BF16),
        vmem((16 * ROOM, RANK), BF16),
        vmem((CHUNKS, 2 * Z, ROOM, CHUNK), F32),
        vmem((CHUNKS, 2 * Z, ROOM, CHUNK), F32),
        pltpu.SemaphoreType.DMA((LOCAL,)),
        pltpu.SemaphoreType.DMA((REMOTE,)),
        pltpu.SemaphoreType.DMA((REMOTE,)),
    ]
    anywhere = pl.BlockSpec(memory_space=pl.ANY)
    return pl.pallas_call(
        kernel,
        out_shape=jax.ShapeDtypeStruct((SAMP, VECS), F32),
        in_specs=[pl.BlockSpec(memory_space=pltpu.SMEM)] + [anywhere] * 5,
        out_specs=pl.BlockSpec(memory_space=pltpu.VMEM),
        scratch_shapes=scratch,
        compiler_params=pltpu.CompilerParams(
            collective_id=0, has_side_effects=True, vmem_limit_bytes=56 * 2**20
        ),
        cost_estimate=pl.CostEstimate(
            flops=2 * 1700 * 10**6, bytes_accessed=12 * 2**20, transcendentals=0
        ),
    )(sample_rows, vectors, leaf_in, leaf_out, factors, dense_rows)


def solution(mesh):
    return jax.shard_map(
        per_device,
        mesh=mesh,
        in_specs=(
            P(("grp", "lvl"), None),
            P(None, ("grp", "lvl")),
            P(("grp", "lvl"), None),
            P(("grp", "lvl"), None, None, None, None),
            P(None, ("grp", "lvl")),
            P(("grp", "lvl")),
        ),
        out_specs=P(("grp", "lvl"), None),
        check_vma=False,
    )
```

```python
import functools

import jax
import jax.numpy as jnp
from jax import lax
from jax.experimental import pallas as pl
from jax.experimental.pallas import tpu as pltpu
from jax.sharding import PartitionSpec as P

MESH = pl.DeviceIdType.MESH
BF16, F32 = jnp.bfloat16, jnp.float32

ROWS, RANK, VECS, SAMP = 2048, 256, 384, 6
Z, X, Y = 8, 4, 4
BLOCK = Z * SAMP
HALF = Y * BLOCK
CHUNK = 128
CHUNKS = VECS // CHUNK
ROOM = 8
GROUPS = (0, 4, 2, 6, 1, 5, 3, 7)


def dot(a, b):
    return jnp.dot(a, b, preferred_element_type=F32)


def dot16(a, b):
    return dot(a, b).astype(BF16)


def count_steps(values, step, steps):
    total = jnp.zeros_like(values)
    for i in range(1, steps):
        total = total + (values >= i * step).astype(jnp.int32)
    return total


def permutation(core, y):
    row = lax.broadcasted_iota(jnp.int32, (2 * HALF, 1), 0)
    half = count_steps(row, HALF, 2)
    row = row - half * HALF
    quarter = count_steps(row, BLOCK, Y)
    row = row - quarter * BLOCK
    z = count_steps(row, SAMP, Z)
    sample = row - z * SAMP
    source = z * BLOCK + (quarter ^ y) * (2 * SAMP) + (half ^ core) * SAMP + sample
    column = lax.broadcasted_iota(jnp.int32, (2 * HALF, 2 * HALF), 1)
    return jnp.where(column == source, 1.0, 0.0).astype(BF16)


def spread(z):
    row = lax.broadcasted_iota(jnp.int32, (Z * ROOM, 1), 0)
    group = count_steps(row, ROOM, Z)
    sample = row - group * ROOM
    offset = jnp.zeros_like(group)
    for i, value in enumerate(GROUPS):
        offset = offset + jnp.where(group == i, value, 0)
    source = jnp.where(sample < SAMP, (offset ^ z) * SAMP + sample, -1)
    column = lax.broadcasted_iota(jnp.int32, (Z * ROOM, BLOCK), 1)
    return jnp.where(column == source, 1.0, 0.0).astype(BF16)


def kernel(
    samp, vec_hbm, lin_hbm, lout_hbm, fac_hbm, dense_hbm, out,
    vec, lin, lout, fac, dense, perm,
    c0_send, c0_recv, c1, c1_recv, c2, c2_recv, c3, c3_recv,
    half_send, half_recv, mine, xs_send, xs_recv, ys_send, ys_recv, total_y,
    w_send4, w_recv4, w_send2, w_recv2, w_send1, w_recv1, w_send_x, w_recv_x, w_all,
    tail_send, tail_recv, last_send, last_recv, local_sem, send_sem, recv_sem,
):
    z, lvl = lax.axis_index("grp"), lax.axis_index("lvl")
    x, y, core = lvl // 8, (lvl // 2) % 4, lvl % 2

    def core_peer():
        return (z, lvl ^ 1)

    def y_peer(j):
        return (z, lvl ^ (2 * j))

    def x_peer(j):
        return (z, lvl ^ (8 * j))

    def z_peer(j):
        return (z ^ j, lvl)

    def tail_peer(i):
        return (z ^ GROUPS[i % Z], lvl ^ (16 * (i // Z)))

    peers = [core_peer()] + [y_peer(j) for j in (1, 2, 3)] + [x_peer(j) for j in (1, 2, 3)]
    peers += [tail_peer(i) for i in range(1, Z)]
    barrier = pltpu.get_barrier_semaphore()
    for peer in peers[::-1]:
        pl.semaphore_signal(barrier, inc=1, device_id=peer, device_id_type=MESH)

    used = [0, 0]
    sent = []

    def load(source, target):
        copy = pltpu.make_async_copy(source, target, local_sem.at[used[0]])
        used[0] += 1
        copy.start()
        return copy

    def send(source, target, peer):
        copy = pltpu.make_async_remote_copy(
            src_ref=source,
            dst_ref=target,
            send_sem=send_sem.at[used[1]],
            recv_sem=recv_sem.at[used[1]],
            device_id=peer,
            device_id_type=MESH,
        )
        used[1] += 1
        copy.start()
        sent.append(copy)
        return copy

    def load_factors(level):
        return load(fac_hbm.at[0, level], fac.at[level])

    def load_dense(j):
        copies = []
        for group in range(Z):
            first = pl.multiple_of(group * (X * BLOCK) + (x ^ j) * BLOCK, BLOCK)
            copies.append(
                load(dense_hbm.at[pl.ds(first, BLOCK), :], dense.at[j, pl.ds(group * BLOCK, BLOCK), :])
            )
        return copies

    got_lin, got_vec = load(lin_hbm, lin), load(vec_hbm, vec)
    got_lout = load(lout_hbm, lout)
    got_fac = {7: load_factors(7)}
    got_fac[0] = load_factors(0)
    got_dense = {}
    order = (2, 1, 3, 0)
    for j in order[:2]:
        got_dense[j] = load_dense(j)
    got_fac[1] = load_factors(1)
    got_fac[6] = load_factors(6)
    for j in order[2:]:
        got_dense[j] = load_dense(j)
    for level in (2, 5, 3, 4):
        got_fac[level] = load_factors(level)

    column = lax.broadcasted_iota(jnp.int32, (2 * ROOM, ROWS), 1)
    row = lax.broadcasted_iota(jnp.int32, (2 * ROOM, ROWS), 0)
    hot = jnp.zeros((2 * ROOM, ROWS), F32)
    for i in range(SAMP):
        hot = jnp.where((row == i) & (column == samp[i]), 1.0, hot)
    hot = hot.astype(BF16)
    perm[...] = permutation(core, y)

    got_lin.wait()
    got_vec.wait()
    c0_send[...] = dot16(lin[...], vec[...])

    got_lout.wait()
    w = dot16(hot, lout[...])
    got_fac[7].wait()
    w_send4[...] = dot16(w, fac[7, 1])
    own4 = dot(w, fac[7, 0])[:ROOM]

    pl.semaphore_wait(barrier, len(peers))
    move4 = send(w_send4, w_recv4, z_peer(4))
    move_c0 = send(c0_send, c0_recv, core_peer())

    def dense_product(j):
        for copy in got_dense[j]:
            copy.wait()
        product = dot16(dense[j], vec[...])
        product = dot(perm[...], product)
        mine[j] = product[:HALF]
        half_send[j] = product[HALF:].astype(BF16)
        return send(half_send.at[j], half_recv.at[j], core_peer())

    move_half = {2: dense_product(2)}
    got_fac[0].wait()
    near = dot(fac[0, 0], c0_send[...])
    move_c0.wait_recv()
    c1[...] = (near + dot(fac[0, 1], c0_recv[...])).astype(BF16)

    columns = [pl.ds(k * CHUNK, CHUNK) for k in range(CHUNKS)]

    def exchange(k, ref, landing, peer):
        return send(ref.at[:, columns[k]], landing.at[:, columns[k]], peer)

    def combine(level, k, ref, landing, move, result):
        near = dot(fac[level, 0], ref[:, columns[k]])
        move.wait_recv()
        far = dot(fac[level, 1], landing[:, columns[k]])
        result[:, columns[k]] = (near + far).astype(BF16)

    def send_half(j):
        move_half[j].wait_recv()
        xs_send[j - 1] = (mine[j] + half_recv[j].astype(F32)).astype(BF16)
        return send(xs_send.at[j - 1], xs_recv.at[j - 1], x_peer(j))

    move_c1 = [exchange(k, c1, c1_recv, y_peer(1)) for k in range(CHUNKS)]
    move_xs, move_c2, move_c3 = {}, {}, {}
    move_half[1] = dense_product(1)
    move_xs[2] = send_half(2)
    move_half[3] = dense_product(3)
    move_xs[1] = send_half(1)
    move_half[0] = dense_product(0)
    move_xs[3] = send_half(3)

    got_fac[1].wait()
    combine(1, 0, c1, c1_recv, move_c1[0], c2)
    move_c2[0] = exchange(0, c2, c2_recv, y_peer(2))

    got_fac[6].wait()
    move4.wait_recv()
    w = jnp.concatenate([own4, w_recv4[...].astype(F32)[:ROOM]], axis=0).astype(BF16)
    w_send2[...] = dot16(w, fac[6, 1])
    move2 = send(w_send2, w_recv2, z_peer(2))
    own2 = dot16(w, fac[6, 0])

    for k in range(1, CHUNKS):
        combine(1, k, c1, c1_recv, move_c1[k], c2)
        move_c2[k] = exchange(k, c2, c2_recv, y_peer(2))

    got_fac[5].wait()
    move2.wait_recv()
    w = jnp.concatenate([own2, w_recv2[...]], axis=0)
    w_send1[...] = dot16(w, fac[5, 1])
    move1 = send(w_send1, w_recv1, z_peer(1))
    own1 = dot16(w, fac[5, 0])

    got_fac[2].wait()
    combine(2, 0, c2, c2_recv, move_c2[0], c3)
    move_c3[0] = exchange(0, c3, c3_recv, x_peer(1))

    got_fac[4].wait()
    move1.wait_recv()
    w = jnp.concatenate([own1, w_recv1[...]], axis=0)
    w_send_x[...] = dot16(w, fac[4, 1])
    move_x = send(w_send_x, w_recv_x, x_peer(2))
    w_all[: Z * ROOM] = dot16(w, fac[4, 0])

    combine(2, 1, c2, c2_recv, move_c2[1], c3)
    move_c3[1] = exchange(1, c3, c3_recv, x_peer(1))

    combine(2, 2, c2, c2_recv, move_c2[2], c3)
    move_c3[2] = exchange(2, c3, c3_recv, x_peer(1))

    move_half[0].wait_recv()
    total = mine[0] + half_recv[0].astype(F32)
    for j in (1, 2, 3):
        move_xs[j].wait_recv()
        total = total + xs_recv[j - 1].astype(F32)
    total_y[...] = total[:BLOCK]
    move_ys = {}
    for j in (1, 2, 3):
        ys_send[j - 1] = total[j * BLOCK : (j + 1) * BLOCK].astype(BF16)
        move_ys[j] = send(ys_send.at[j - 1], ys_recv.at[j - 1], y_peer(j))

    got_fac[3].wait()
    onto = spread(z)
    move_x.wait_recv()
    w_all[Z * ROOM :] = w_recv_x[...]
    w = w_all[...]

    move_tail = {}

    def send_tail(k, i):
        move_tail[k, i] = send(tail_send.at[k, i], tail_recv.at[k, i], tail_peer(Z + i))

    for k in range(CHUNKS):
        near = dot(fac[3, 0], c3[:, columns[k]])
        move_c3[k].wait_recv()
        far = dot(fac[3, 1], c3_recv[:, columns[k]])
        part = dot(w, (near + far).astype(BF16))
        last_send[:, columns[k]] = part[: Z * ROOM]
        for i in range(Z):
            tail_send[k, i] = part[(Z + i) * ROOM : (Z + i + 1) * ROOM]
            send_tail(k, i)

    total = total_y[...]
    for j in (1, 2, 3):
        move_ys[j].wait_recv()
        total = total + ys_recv[j - 1].astype(F32)
    high = total.astype(BF16)
    low = (total - high.astype(F32)).astype(BF16)
    exact = dot(onto, high) + dot(onto, low)
    last_send[...] = last_send[...] - exact
    move_last = {}
    for i in range(1, Z):
        rows = pl.ds(i * ROOM, ROOM)
        move_last[i] = send(last_send.at[rows, :], last_recv.at[rows, :], tail_peer(i))

    for copy in sent:
        copy.wait_send()
    for k in range(CHUNKS):
        part = last_send[:ROOM, columns[k]]
        for i in range(Z):
            move_tail[k, i].wait_recv()
            part = part + tail_recv[k, i]
        total_y[:ROOM, columns[k]] = part
    part = total_y[:ROOM, :]
    for i in range(1, Z):
        move_last[i].wait_recv()
        part = part + last_recv[i * ROOM : (i + 1) * ROOM, :]
    out[...] = part[:SAMP]


LOCAL = 3 + 8 + Z * X
REMOTE = 1 + 3 * CHUNKS + 4 + 3 + 3 + 4 + Z * CHUNKS + Z - 1


def per_device(vectors, leaf_in, leaf_out, factors, dense_rows, sample_rows):
    vmem = pltpu.VMEM
    scratch = [
        vmem((ROWS, VECS), BF16),
        vmem((RANK, ROWS), BF16),
        vmem((ROWS, RANK), BF16),
        vmem((8, 2, RANK, RANK), BF16),
        vmem((X, 2 * HALF, ROWS), BF16),
        vmem((2 * HALF, 2 * HALF), BF16),
        vmem((RANK, VECS), BF16),
        vmem((RANK, VECS), BF16),
        vmem((RANK, VECS), BF16),
        vmem((RANK, VECS), BF16),
        vmem((RANK, VECS), BF16),
        vmem((RANK, VECS), BF16),
        vmem((RANK, VECS), BF16),
        vmem((RANK, VECS), BF16),
        vmem((X, HALF, VECS), BF16),
        vmem((X, HALF, VECS), BF16),
        vmem((X, HALF, VECS), F32),
        vmem((3, HALF, VECS), BF16),
        vmem((3, HALF, VECS), BF16),
        vmem((3, BLOCK, VECS), BF16),
        vmem((3, BLOCK, VECS), BF16),
        vmem((BLOCK, VECS), F32),
        vmem((2 * ROOM, RANK), BF16),
        vmem((2 * ROOM, RANK), BF16),
        vmem((2 * ROOM, RANK), BF16),
        vmem((2 * ROOM, RANK), BF16),
        vmem((4 * ROOM, RANK), BF16),
        vmem((4 * ROOM, RANK), BF16),
        vmem((8 * ROOM, RANK), BF16),
        vmem((8 * ROOM, RANK), BF16),
        vmem((16 * ROOM, RANK), BF16),
        vmem((CHUNKS, Z, ROOM, CHUNK), F32),
        vmem((CHUNKS, Z, ROOM, CHUNK), F32),
        vmem((Z * ROOM, VECS), F32),
        vmem((Z * ROOM, VECS), F32),
        pltpu.SemaphoreType.DMA((LOCAL,)),
        pltpu.SemaphoreType.DMA((REMOTE,)),
        pltpu.SemaphoreType.DMA((REMOTE,)),
    ]
    anywhere = pl.BlockSpec(memory_space=pl.ANY)
    return pl.pallas_call(
        kernel,
        out_shape=jax.ShapeDtypeStruct((SAMP, VECS), F32),
        in_specs=[pl.BlockSpec(memory_space=pltpu.SMEM)] + [anywhere] * 5,
        out_specs=pl.BlockSpec(memory_space=pltpu.VMEM),
        scratch_shapes=scratch,
        compiler_params=pltpu.CompilerParams(
            collective_id=0, has_side_effects=True, vmem_limit_bytes=56 * 2**20
        ),
        cost_estimate=pl.CostEstimate(
            flops=2 * 1700 * 10**6, bytes_accessed=12 * 2**20, transcendentals=0
        ),
    )(sample_rows, vectors, leaf_in, leaf_out, factors, dense_rows)


def solution(mesh):
    return jax.shard_map(
        per_device,
        mesh=mesh,
        in_specs=(
            P(("grp", "lvl"), None),
            P(None, ("grp", "lvl")),
            P(("grp", "lvl"), None),
            P(("grp", "lvl"), None, None, None, None),
            P(None, ("grp", "lvl")),
            P(("grp", "lvl")),
        ),
        out_specs=P(("grp", "lvl"), None),
        check_vma=False,
    )
```

```python
import functools

import jax
import jax.numpy as jnp
from jax import lax
from jax.experimental import pallas as pl
from jax.experimental.pallas import tpu as pltpu
from jax.sharding import PartitionSpec as P

MESH = pl.DeviceIdType.MESH
BF16, F32 = jnp.bfloat16, jnp.float32

ROWS, RANK, VECS, SAMP = 2048, 256, 384, 6
Z, X, Y = 8, 4, 4
BLOCK = Z * SAMP
HALF = Y * BLOCK
CHUNK = 128
CHUNKS = VECS // CHUNK
ROOM = 8
GROUPS = (0, 4, 2, 6, 1, 5, 3, 7)


def dot(a, b):
    return jnp.dot(a, b, preferred_element_type=F32)


def dot16(a, b):
    return dot(a, b).astype(BF16)


def count_steps(values, step, steps):
    total = jnp.zeros_like(values)
    for i in range(1, steps):
        total = total + (values >= i * step).astype(jnp.int32)
    return total


def permutation(core, y):
    row = lax.broadcasted_iota(jnp.int32, (2 * HALF, 1), 0)
    half = count_steps(row, HALF, 2)
    row = row - half * HALF
    quarter = count_steps(row, BLOCK, Y)
    row = row - quarter * BLOCK
    z = count_steps(row, SAMP, Z)
    sample = row - z * SAMP
    source = z * BLOCK + (quarter ^ y) * (2 * SAMP) + (half ^ core) * SAMP + sample
    column = lax.broadcasted_iota(jnp.int32, (2 * HALF, 2 * HALF), 1)
    return jnp.where(column == source, 1.0, 0.0).astype(BF16)


def spread(z):
    row = lax.broadcasted_iota(jnp.int32, (Z * ROOM, 1), 0)
    group = count_steps(row, ROOM, Z)
    sample = row - group * ROOM
    offset = jnp.zeros_like(group)
    for i, value in enumerate(GROUPS):
        offset = offset + jnp.where(group == i, value, 0)
    source = jnp.where(sample < SAMP, (offset ^ z) * SAMP + sample, -1)
    column = lax.broadcasted_iota(jnp.int32, (Z * ROOM, BLOCK), 1)
    return jnp.where(column == source, 1.0, 0.0).astype(BF16)


def kernel(
    samp_hbm, vec_hbm, lin_hbm, lout_hbm, fac_hbm, dense_hbm, out,
    vec, lin, lout, fac, dense, perm,
    c0_send, c0_recv, c1, c1_recv, c2, c2_recv, c3, c3_recv,
    half_send, half_recv, mine, xs_send, xs_recv, ys_send, ys_recv, total_y,
    w_send4, w_recv4, w_send2, w_recv2, w_send1, w_recv1, w_send_x, w_recv_x, w_all,
    tail_send, tail_recv, last_send, last_recv, samp, local_sem, send_sem, recv_sem,
):
    z, lvl = lax.axis_index("grp"), lax.axis_index("lvl")
    x, y, core = lvl // 8, (lvl // 2) % 4, lvl % 2

    def core_peer():
        return (z, lvl ^ 1)

    def y_peer(j):
        return (z, lvl ^ (2 * j))

    def x_peer(j):
        return (z, lvl ^ (8 * j))

    def z_peer(j):
        return (z ^ j, lvl)

    def tail_peer(i):
        return (z ^ GROUPS[i % Z], lvl ^ (16 * (i // Z)))

    peers = [core_peer()] + [y_peer(j) for j in (1, 2, 3)] + [x_peer(j) for j in (1, 2, 3)]
    peers += [tail_peer(i) for i in range(1, Z)]
    barrier = pltpu.get_barrier_semaphore()
    for peer in peers[::-1]:
        pl.semaphore_signal(barrier, inc=1, device_id=peer, device_id_type=MESH)

    used = [0, 0]
    sent = []

    def load(source, target):
        copy = pltpu.make_async_copy(source, target, local_sem.at[used[0]])
        used[0] += 1
        copy.start()
        return copy

    def send(source, target, peer):
        copy = pltpu.make_async_remote_copy(
            src_ref=source,
            dst_ref=target,
            send_sem=send_sem.at[used[1]],
            recv_sem=recv_sem.at[used[1]],
            device_id=peer,
            device_id_type=MESH,
        )
        used[1] += 1
        copy.start()
        sent.append(copy)
        return copy

    def load_factors(level):
        return load(fac_hbm.at[0, level], fac.at[level])

    def load_dense(j):
        copies = []
        for group in range(Z):
            first = pl.multiple_of(group * (X * BLOCK) + (x ^ j) * BLOCK, BLOCK)
            copies.append(
                load(dense_hbm.at[pl.ds(first, BLOCK), :], dense.at[j, pl.ds(group * BLOCK, BLOCK), :])
            )
        return copies

    got_samp = load(samp_hbm, samp)
    got_lin, got_vec = load(lin_hbm, lin), load(vec_hbm, vec)
    got_lout = load(lout_hbm, lout)
    got_fac = {7: load_factors(7)}
    got_fac[0] = load_factors(0)
    got_dense = {}
    order = (2, 1, 3, 0)
    for j in order[:2]:
        got_dense[j] = load_dense(j)
    got_fac[1] = load_factors(1)
    got_fac[6] = load_factors(6)
    for j in order[2:]:
        got_dense[j] = load_dense(j)
    for level in (2, 5, 3, 4):
        got_fac[level] = load_factors(level)

    perm[...] = permutation(core, y)
    got_samp.wait()
    column = lax.broadcasted_iota(jnp.int32, (2 * ROOM, ROWS), 1)
    row = lax.broadcasted_iota(jnp.int32, (2 * ROOM, ROWS), 0)
    hot = jnp.zeros((2 * ROOM, ROWS), F32)
    for i in range(SAMP):
        hot = jnp.where((row == i) & (column == samp[i]), 1.0, hot)
    hot = hot.astype(BF16)

    got_lin.wait()
    got_vec.wait()
    c0_send[...] = dot16(lin[...], vec[...])

    got_lout.wait()
    w = dot16(hot, lout[...])
    got_fac[7].wait()
    w_send4[...] = dot16(w, fac[7, 1])
    own4 = dot(w, fac[7, 0])[:ROOM]

    pl.semaphore_wait(barrier, len(peers))
    move4 = send(w_send4, w_recv4, z_peer(4))
    move_c0 = send(c0_send, c0_recv, core_peer())

    def dense_product(j):
        for copy in got_dense[j]:
            copy.wait()
        product = dot16(dense[j], vec[...])
        product = dot(perm[...], product)
        mine[j] = product[:HALF]
        half_send[j] = product[HALF:].astype(BF16)
        return send(half_send.at[j], half_recv.at[j], core_peer())

    move_half = {2: dense_product(2)}
    got_fac[0].wait()
    near = dot(fac[0, 0], c0_send[...])
    move_c0.wait_recv()
    c1[...] = (near + dot(fac[0, 1], c0_recv[...])).astype(BF16)

    columns = [pl.ds(k * CHUNK, CHUNK) for k in range(CHUNKS)]

    def exchange(k, ref, landing, peer):
        return send(ref.at[:, columns[k]], landing.at[:, columns[k]], peer)

    def combine(level, k, ref, landing, move, result):
        near = dot(fac[level, 0], ref[:, columns[k]])
        move.wait_recv()
        far = dot(fac[level, 1], landing[:, columns[k]])
        result[:, columns[k]] = (near + far).astype(BF16)

    def send_half(j):
        move_half[j].wait_recv()
        xs_send[j - 1] = (mine[j] + half_recv[j].astype(F32)).astype(BF16)
        return send(xs_send.at[j - 1], xs_recv.at[j - 1], x_peer(j))

    move_c1 = [exchange(k, c1, c1_recv, y_peer(1)) for k in range(CHUNKS)]
    move_xs, move_c2, move_c3 = {}, {}, {}
    move_half[1] = dense_product(1)
    move_xs[2] = send_half(2)
    move_half[3] = dense_product(3)
    move_xs[1] = send_half(1)
    move_half[0] = dense_product(0)
    move_xs[3] = send_half(3)

    got_fac[1].wait()
    combine(1, 0, c1, c1_recv, move_c1[0], c2)
    move_c2[0] = exchange(0, c2, c2_recv, y_peer(2))

    got_fac[6].wait()
    move4.wait_recv()
    w = jnp.concatenate([own4, w_recv4[...].astype(F32)[:ROOM]], axis=0).astype(BF16)
    w_send2[...] = dot16(w, fac[6, 1])
    move2 = send(w_send2, w_recv2, z_peer(2))
    own2 = dot16(w, fac[6, 0])

    for k in range(1, CHUNKS):
        combine(1, k, c1, c1_recv, move_c1[k], c2)
        move_c2[k] = exchange(k, c2, c2_recv, y_peer(2))

    got_fac[5].wait()
    move2.wait_recv()
    w = jnp.concatenate([own2, w_recv2[...]], axis=0)
    w_send1[...] = dot16(w, fac[5, 1])
    move1 = send(w_send1, w_recv1, z_peer(1))
    own1 = dot16(w, fac[5, 0])

    got_fac[2].wait()
    combine(2, 0, c2, c2_recv, move_c2[0], c3)
    move_c3[0] = exchange(0, c3, c3_recv, x_peer(1))

    got_fac[4].wait()
    move1.wait_recv()
    w = jnp.concatenate([own1, w_recv1[...]], axis=0)
    w_send_x[...] = dot16(w, fac[4, 1])
    move_x = send(w_send_x, w_recv_x, x_peer(2))
    w_all[: Z * ROOM] = dot16(w, fac[4, 0])

    combine(2, 1, c2, c2_recv, move_c2[1], c3)
    move_c3[1] = exchange(1, c3, c3_recv, x_peer(1))

    combine(2, 2, c2, c2_recv, move_c2[2], c3)
    move_c3[2] = exchange(2, c3, c3_recv, x_peer(1))

    move_half[0].wait_recv()
    total = mine[0] + half_recv[0].astype(F32)
    for j in (1, 2, 3):
        move_xs[j].wait_recv()
        total = total + xs_recv[j - 1].astype(F32)
    total_y[...] = total[:BLOCK]
    move_ys = {}
    for j in (1, 2, 3):
        ys_send[j - 1] = total[j * BLOCK : (j + 1) * BLOCK].astype(BF16)
        move_ys[j] = send(ys_send.at[j - 1], ys_recv.at[j - 1], y_peer(j))

    got_fac[3].wait()
    onto = spread(z)
    move_x.wait_recv()
    w_all[Z * ROOM :] = w_recv_x[...]
    w = w_all[...]

    move_tail = {}

    def send_tail(k, i):
        move_tail[k, i] = send(tail_send.at[k, i], tail_recv.at[k, i], tail_peer(Z + i))

    for k in range(CHUNKS):
        near = dot(fac[3, 0], c3[:, columns[k]])
        move_c3[k].wait_recv()
        far = dot(fac[3, 1], c3_recv[:, columns[k]])
        part = dot(w, (near + far).astype(BF16))
        last_send[:, columns[k]] = part[: Z * ROOM]
        for i in range(Z):
            tail_send[k, i] = part[(Z + i) * ROOM : (Z + i + 1) * ROOM]
            send_tail(k, i)

    total = total_y[...]
    for j in (1, 2, 3):
        move_ys[j].wait_recv()
        total = total + ys_recv[j - 1].astype(F32)
    high = total.astype(BF16)
    low = (total - high.astype(F32)).astype(BF16)
    exact = dot(onto, high) + dot(onto, low)
    last_send[...] = last_send[...] - exact
    move_last = {}
    for i in range(1, Z):
        rows = pl.ds(i * ROOM, ROOM)
        move_last[i] = send(last_send.at[rows, :], last_recv.at[rows, :], tail_peer(i))

    for copy in sent:
        copy.wait_send()
    for k in range(CHUNKS):
        part = last_send[:ROOM, columns[k]]
        for i in range(Z):
            move_tail[k, i].wait_recv()
            part = part + tail_recv[k, i]
        total_y[:ROOM, columns[k]] = part
    part = total_y[:ROOM, :]
    for i in range(1, Z):
        move_last[i].wait_recv()
        part = part + last_recv[i * ROOM : (i + 1) * ROOM, :]
    out[...] = part[:SAMP]


LOCAL = 4 + 8 + Z * X
REMOTE = 1 + 3 * CHUNKS + 4 + 3 + 3 + 4 + Z * CHUNKS + Z - 1


def per_device(vectors, leaf_in, leaf_out, factors, dense_rows, sample_rows):
    vmem = pltpu.VMEM
    scratch = [
        vmem((ROWS, VECS), BF16),
        vmem((RANK, ROWS), BF16),
        vmem((ROWS, RANK), BF16),
        vmem((8, 2, RANK, RANK), BF16),
        vmem((X, 2 * HALF, ROWS), BF16),
        vmem((2 * HALF, 2 * HALF), BF16),
        vmem((RANK, VECS), BF16),
        vmem((RANK, VECS), BF16),
        vmem((RANK, VECS), BF16),
        vmem((RANK, VECS), BF16),
        vmem((RANK, VECS), BF16),
        vmem((RANK, VECS), BF16),
        vmem((RANK, VECS), BF16),
        vmem((RANK, VECS), BF16),
        vmem((X, HALF, VECS), BF16),
        vmem((X, HALF, VECS), BF16),
        vmem((X, HALF, VECS), F32),
        vmem((3, HALF, VECS), BF16),
        vmem((3, HALF, VECS), BF16),
        vmem((3, BLOCK, VECS), BF16),
        vmem((3, BLOCK, VECS), BF16),
        vmem((BLOCK, VECS), F32),
        vmem((2 * ROOM, RANK), BF16),
        vmem((2 * ROOM, RANK), BF16),
        vmem((2 * ROOM, RANK), BF16),
        vmem((2 * ROOM, RANK), BF16),
        vmem((4 * ROOM, RANK), BF16),
        vmem((4 * ROOM, RANK), BF16),
        vmem((8 * ROOM, RANK), BF16),
        vmem((8 * ROOM, RANK), BF16),
        vmem((16 * ROOM, RANK), BF16),
        vmem((CHUNKS, Z, ROOM, CHUNK), F32),
        vmem((CHUNKS, Z, ROOM, CHUNK), F32),
        vmem((Z * ROOM, VECS), F32),
        vmem((Z * ROOM, VECS), F32),
        pltpu.SMEM((SAMP,), jnp.int32),
        pltpu.SemaphoreType.DMA((LOCAL,)),
        pltpu.SemaphoreType.DMA((REMOTE,)),
        pltpu.SemaphoreType.DMA((REMOTE,)),
    ]
    anywhere = pl.BlockSpec(memory_space=pl.ANY)
    return pl.pallas_call(
        kernel,
        out_shape=pltpu.VMEM((SAMP, VECS), F32),
        in_specs=[anywhere] * 6,
        out_specs=pl.BlockSpec(memory_space=pltpu.VMEM),
        scratch_shapes=scratch,
        compiler_params=pltpu.CompilerParams(
            collective_id=0, has_side_effects=True, vmem_limit_bytes=56 * 2**20
        ),
        cost_estimate=pl.CostEstimate(
            flops=2 * 1700 * 10**6, bytes_accessed=12 * 2**20, transcendentals=0
        ),
    )(sample_rows, vectors, leaf_in, leaf_out, factors, dense_rows)


def solution(mesh):
    return jax.shard_map(
        per_device,
        mesh=mesh,
        in_specs=(
            P(("grp", "lvl"), None),
            P(None, ("grp", "lvl")),
            P(("grp", "lvl"), None),
            P(("grp", "lvl"), None, None, None, None),
            P(None, ("grp", "lvl")),
            P(("grp", "lvl")),
        ),
        out_specs=P(("grp", "lvl"), None),
        check_vma=False,
    )
```

```python
import functools

import jax
import jax.numpy as jnp
from jax import lax
from jax.experimental import pallas as pl
from jax.experimental.pallas import tpu as pltpu
from jax.sharding import PartitionSpec as P

MESH = pl.DeviceIdType.MESH
BF16, F32 = jnp.bfloat16, jnp.float32

ROWS, RANK, VECS, SAMP = 2048, 256, 384, 6
Z, X, Y = 8, 4, 4
BLOCK = Z * SAMP
HALF = Y * BLOCK
CHUNK = 128
CHUNKS = VECS // CHUNK
ROOM = 8
GROUPS = (0, 4, 2, 6, 1, 5, 3, 7)


def dot(a, b):
    return jnp.dot(a, b, preferred_element_type=F32)


def dot16(a, b):
    return dot(a, b).astype(BF16)


def count_steps(values, step, steps):
    total = jnp.zeros_like(values)
    for i in range(1, steps):
        total = total + (values >= i * step).astype(jnp.int32)
    return total


def permutation(core, y):
    row = lax.broadcasted_iota(jnp.int32, (2 * HALF, 1), 0)
    half = count_steps(row, HALF, 2)
    row = row - half * HALF
    quarter = count_steps(row, BLOCK, Y)
    row = row - quarter * BLOCK
    z = count_steps(row, SAMP, Z)
    sample = row - z * SAMP
    source = z * BLOCK + (quarter ^ y) * (2 * SAMP) + (half ^ core) * SAMP + sample
    column = lax.broadcasted_iota(jnp.int32, (2 * HALF, 2 * HALF), 1)
    return jnp.where(column == source, 1.0, 0.0).astype(BF16)


def spread(z):
    row = lax.broadcasted_iota(jnp.int32, (Z * ROOM, 1), 0)
    group = count_steps(row, ROOM, Z)
    sample = row - group * ROOM
    offset = jnp.zeros_like(group)
    for i, value in enumerate(GROUPS):
        offset = offset + jnp.where(group == i, value, 0)
    source = jnp.where(sample < SAMP, (offset ^ z) * SAMP + sample, -1)
    column = lax.broadcasted_iota(jnp.int32, (Z * ROOM, BLOCK), 1)
    return jnp.where(column == source, 1.0, 0.0).astype(BF16)


def kernel(
    samp_hbm, vec_hbm, lin_hbm, lout_hbm, fac_hbm, dense_hbm, out,
    vec, lin, lout, fac, dense, perm,
    c0_send, c0_recv, c1, c1_recv, c2, c2_recv, c3, c3_recv,
    half_send, half_recv, mine, xs_send, xs_recv, ys_send, ys_recv, total_y,
    w_send4, w_recv4, w_send2, w_recv2, w_send1, w_recv1, w_send_x, w_recv_x, w_all,
    tail_send, tail_recv, last_send, last_recv, samp, local_sem, send_sem, recv_sem,
):
    z, lvl = lax.axis_index("grp"), lax.axis_index("lvl")
    x, y, core = lvl // 8, (lvl // 2) % 4, lvl % 2

    def core_peer():
        return (z, lvl ^ 1)

    def y_peer(j):
        return (z, lvl ^ (2 * j))

    def x_peer(j):
        return (z, lvl ^ (8 * j))

    def z_peer(j):
        return (z ^ j, lvl)

    def tail_peer(i):
        return (z ^ GROUPS[i % Z], lvl ^ (16 * (i // Z)))

    peers = [core_peer()] + [y_peer(j) for j in (1, 2, 3)] + [x_peer(j) for j in (1, 2, 3)]
    peers += [tail_peer(i) for i in range(1, Z)]
    barrier = pltpu.get_barrier_semaphore()
    for peer in peers[::-1]:
        pl.semaphore_signal(barrier, inc=1, device_id=peer, device_id_type=MESH)

    used = [0, 0]
    sent = []

    def load(source, target):
        copy = pltpu.make_async_copy(source, target, local_sem.at[used[0]])
        used[0] += 1
        copy.start()
        return copy

    def send(source, target, peer):
        copy = pltpu.make_async_remote_copy(
            src_ref=source,
            dst_ref=target,
            send_sem=send_sem.at[used[1]],
            recv_sem=recv_sem.at[used[1]],
            device_id=peer,
            device_id_type=MESH,
        )
        used[1] += 1
        copy.start()
        sent.append(copy)
        return copy

    def load_factors(level):
        return load(fac_hbm.at[0, level], fac.at[level])

    order = (2, 1, 3, 0)

    def load_dense(j):
        copies = []
        for group in range(Z):
            first = pl.multiple_of(group * (X * BLOCK) + (x ^ j) * BLOCK, BLOCK)
            copies.append(
                load(dense_hbm.at[pl.ds(first, BLOCK), :], dense.at[order.index(j), pl.ds(group * BLOCK, BLOCK), :])
            )
        return copies

    got_samp = load(samp_hbm, samp)
    got_lin, got_vec = load(lin_hbm, lin), load(vec_hbm, vec)
    got_lout = load(lout_hbm, lout)
    got_fac = {7: load_factors(7)}
    got_fac[0] = load_factors(0)
    got_dense = {}
    for j in order[:2]:
        got_dense[j] = load_dense(j)
    got_fac[1] = load_factors(1)
    got_fac[6] = load_factors(6)
    for j in order[2:]:
        got_dense[j] = load_dense(j)
    for level in (2, 5, 3, 4):
        got_fac[level] = load_factors(level)

    perm[...] = permutation(core, y)
    got_samp.wait()
    column = lax.broadcasted_iota(jnp.int32, (2 * ROOM, ROWS), 1)
    row = lax.broadcasted_iota(jnp.int32, (2 * ROOM, ROWS), 0)
    hot = jnp.zeros((2 * ROOM, ROWS), F32)
    for i in range(SAMP):
        hot = jnp.where((row == i) & (column == samp[i]), 1.0, hot)
    hot = hot.astype(BF16)

    got_lin.wait()
    got_vec.wait()
    c0_send[...] = dot16(lin[...], vec[...])

    got_lout.wait()
    w = dot16(hot, lout[...])
    got_fac[7].wait()
    w_send4[...] = dot16(w, fac[7, 1])
    own4 = dot(w, fac[7, 0])[:ROOM]

    pl.semaphore_wait(barrier, len(peers))
    move4 = send(w_send4, w_recv4, z_peer(4))
    move_c0 = send(c0_send, c0_recv, core_peer())

    def dense_products(first, blocks):
        for j in blocks:
            for copy in got_dense[j]:
                copy.wait()
        rows = dense[first : first + len(blocks)].reshape(len(blocks) * 2 * HALF, ROWS)
        products = dot16(rows, vec[...])
        for i, j in enumerate(blocks):
            product = dot(perm[...], products[i * 2 * HALF : (i + 1) * 2 * HALF])
            mine[j] = product[:HALF]
            half_send[j] = product[HALF:].astype(BF16)
            move_half[j] = send(half_send.at[j], half_recv.at[j], core_peer())

    move_half = {}
    dense_products(0, (2,))
    got_fac[0].wait()
    near = dot(fac[0, 0], c0_send[...])
    move_c0.wait_recv()
    c1[...] = (near + dot(fac[0, 1], c0_recv[...])).astype(BF16)

    columns = [pl.ds(k * CHUNK, CHUNK) for k in range(CHUNKS)]

    def exchange(k, ref, landing, peer):
        return send(ref.at[:, columns[k]], landing.at[:, columns[k]], peer)

    def combine(level, k, ref, landing, move, result):
        near = dot(fac[level, 0], ref[:, columns[k]])
        move.wait_recv()
        far = dot(fac[level, 1], landing[:, columns[k]])
        result[:, columns[k]] = (near + far).astype(BF16)

    def send_half(j):
        move_half[j].wait_recv()
        xs_send[j - 1] = (mine[j] + half_recv[j].astype(F32)).astype(BF16)
        return send(xs_send.at[j - 1], xs_recv.at[j - 1], x_peer(j))

    move_c1 = [exchange(k, c1, c1_recv, y_peer(1)) for k in range(CHUNKS)]
    move_xs, move_c2, move_c3 = {}, {}, {}
    dense_products(1, (1, 3))
    move_xs[2] = send_half(2)
    dense_products(3, (0,))
    move_xs[1] = send_half(1)
    move_xs[3] = send_half(3)

    got_fac[1].wait()
    combine(1, 0, c1, c1_recv, move_c1[0], c2)
    move_c2[0] = exchange(0, c2, c2_recv, y_peer(2))

    got_fac[6].wait()
    move4.wait_recv()
    w = jnp.concatenate([own4, w_recv4[...].astype(F32)[:ROOM]], axis=0).astype(BF16)
    w_send2[...] = dot16(w, fac[6, 1])
    move2 = send(w_send2, w_recv2, z_peer(2))
    own2 = dot16(w, fac[6, 0])

    for k in range(1, CHUNKS):
        combine(1, k, c1, c1_recv, move_c1[k], c2)
        move_c2[k] = exchange(k, c2, c2_recv, y_peer(2))

    got_fac[5].wait()
    move2.wait_recv()
    w = jnp.concatenate([own2, w_recv2[...]], axis=0)
    w_send1[...] = dot16(w, fac[5, 1])
    move1 = send(w_send1, w_recv1, z_peer(1))
    own1 = dot16(w, fac[5, 0])

    got_fac[2].wait()
    combine(2, 0, c2, c2_recv, move_c2[0], c3)
    move_c3[0] = exchange(0, c3, c3_recv, x_peer(1))

    got_fac[4].wait()
    move1.wait_recv()
    w = jnp.concatenate([own1, w_recv1[...]], axis=0)
    w_send_x[...] = dot16(w, fac[4, 1])
    move_x = send(w_send_x, w_recv_x, x_peer(2))
    w_all[: Z * ROOM] = dot16(w, fac[4, 0])

    combine(2, 1, c2, c2_recv, move_c2[1], c3)
    move_c3[1] = exchange(1, c3, c3_recv, x_peer(1))

    combine(2, 2, c2, c2_recv, move_c2[2], c3)
    move_c3[2] = exchange(2, c3, c3_recv, x_peer(1))

    move_half[0].wait_recv()
    total = mine[0] + half_recv[0].astype(F32)
    for j in (1, 2, 3):
        move_xs[j].wait_recv()
        total = total + xs_recv[j - 1].astype(F32)
    total_y[...] = total[:BLOCK]
    move_ys = {}
    for j in (1, 2, 3):
        ys_send[j - 1] = total[j * BLOCK : (j + 1) * BLOCK].astype(BF16)
        move_ys[j] = send(ys_send.at[j - 1], ys_recv.at[j - 1], y_peer(j))

    got_fac[3].wait()
    onto = spread(z)
    move_x.wait_recv()
    w_all[Z * ROOM :] = w_recv_x[...]
    w = w_all[...]

    move_tail = {}

    def send_tail(k, i):
        move_tail[k, i] = send(tail_send.at[k, i], tail_recv.at[k, i], tail_peer(Z + i))

    for k in range(CHUNKS):
        near = dot(fac[3, 0], c3[:, columns[k]])
        move_c3[k].wait_recv()
        far = dot(fac[3, 1], c3_recv[:, columns[k]])
        part = dot(w, (near + far).astype(BF16))
        last_send[:, columns[k]] = part[: Z * ROOM]
        for i in range(Z):
            tail_send[k, i] = part[(Z + i) * ROOM : (Z + i + 1) * ROOM]
            send_tail(k, i)

    total = total_y[...]
    for j in (1, 2, 3):
        move_ys[j].wait_recv()
        total = total + ys_recv[j - 1].astype(F32)
    high = total.astype(BF16)
    low = (total - high.astype(F32)).astype(BF16)
    exact = dot(onto, high) + dot(onto, low)
    last_send[...] = last_send[...] - exact
    move_last = {}
    for i in range(1, Z):
        rows = pl.ds(i * ROOM, ROOM)
        move_last[i] = send(last_send.at[rows, :], last_recv.at[rows, :], tail_peer(i))

    for copy in sent:
        copy.wait_send()
    for k in range(CHUNKS):
        part = last_send[:ROOM, columns[k]]
        for i in range(Z):
            move_tail[k, i].wait_recv()
            part = part + tail_recv[k, i]
        total_y[:ROOM, columns[k]] = part
    part = total_y[:ROOM, :]
    for i in range(1, Z):
        move_last[i].wait_recv()
        part = part + last_recv[i * ROOM : (i + 1) * ROOM, :]
    out[...] = part[:SAMP]


LOCAL = 4 + 8 + Z * X
REMOTE = 1 + 3 * CHUNKS + 4 + 3 + 3 + 4 + Z * CHUNKS + Z - 1


def per_device(vectors, leaf_in, leaf_out, factors, dense_rows, sample_rows):
    vmem = pltpu.VMEM
    scratch = [
        vmem((ROWS, VECS), BF16),
        vmem((RANK, ROWS), BF16),
        vmem((ROWS, RANK), BF16),
        vmem((8, 2, RANK, RANK), BF16),
        vmem((X, 2 * HALF, ROWS), BF16),
        vmem((2 * HALF, 2 * HALF), BF16),
        vmem((RANK, VECS), BF16),
        vmem((RANK, VECS), BF16),
        vmem((RANK, VECS), BF16),
        vmem((RANK, VECS), BF16),
        vmem((RANK, VECS), BF16),
        vmem((RANK, VECS), BF16),
        vmem((RANK, VECS), BF16),
        vmem((RANK, VECS), BF16),
        vmem((X, HALF, VECS), BF16),
        vmem((X, HALF, VECS), BF16),
        vmem((X, HALF, VECS), F32),
        vmem((3, HALF, VECS), BF16),
        vmem((3, HALF, VECS), BF16),
        vmem((3, BLOCK, VECS), BF16),
        vmem((3, BLOCK, VECS), BF16),
        vmem((BLOCK, VECS), F32),
        vmem((2 * ROOM, RANK), BF16),
        vmem((2 * ROOM, RANK), BF16),
        vmem((2 * ROOM, RANK), BF16),
        vmem((2 * ROOM, RANK), BF16),
        vmem((4 * ROOM, RANK), BF16),
        vmem((4 * ROOM, RANK), BF16),
        vmem((8 * ROOM, RANK), BF16),
        vmem((8 * ROOM, RANK), BF16),
        vmem((16 * ROOM, RANK), BF16),
        vmem((CHUNKS, Z, ROOM, CHUNK), F32),
        vmem((CHUNKS, Z, ROOM, CHUNK), F32),
        vmem((Z * ROOM, VECS), F32),
        vmem((Z * ROOM, VECS), F32),
        pltpu.SMEM((SAMP,), jnp.int32),
        pltpu.SemaphoreType.DMA((LOCAL,)),
        pltpu.SemaphoreType.DMA((REMOTE,)),
        pltpu.SemaphoreType.DMA((REMOTE,)),
    ]
    anywhere = pl.BlockSpec(memory_space=pl.ANY)
    return pl.pallas_call(
        kernel,
        out_shape=pltpu.VMEM((SAMP, VECS), F32),
        in_specs=[anywhere] * 6,
        out_specs=pl.BlockSpec(memory_space=pltpu.VMEM),
        scratch_shapes=scratch,
        compiler_params=pltpu.CompilerParams(
            collective_id=0, has_side_effects=True, vmem_limit_bytes=56 * 2**20
        ),
        cost_estimate=pl.CostEstimate(
            flops=2 * 1700 * 10**6, bytes_accessed=12 * 2**20, transcendentals=0
        ),
    )(sample_rows, vectors, leaf_in, leaf_out, factors, dense_rows)


def solution(mesh):
    return jax.shard_map(
        per_device,
        mesh=mesh,
        in_specs=(
            P(("grp", "lvl"), None),
            P(None, ("grp", "lvl")),
            P(("grp", "lvl"), None),
            P(("grp", "lvl"), None, None, None, None),
            P(None, ("grp", "lvl")),
            P(("grp", "lvl")),
        ),
        out_specs=P(("grp", "lvl"), None),
        check_vma=False,
    )
```
